32 devices in a mesh: groups: 2 (over x), sub: 16 (over z, y, core).
Axes of the slice: x: 2, y: 2, z: 4, core: 2. Of those that a mesh axis runs over, the one named last changes fastest.
Arguments:
- rhs: float32 [32, 196608], P('groups', 'sub'), parts along dimension 0, may hold values from -8 to 8
- mass: float32 [393216], P(('groups', 'sub')), parts along dimension 0, may hold values from 0.5 to 2
- jacobi: float32 [393216], P(('groups', 'sub')), parts along dimension 0, may hold values from 0.1 to 1
- local_edges: int32 [2, 12288], P(None, ('groups', 'sub')), parts along dimension 1, may hold values from 0 to 191, as said below
- local_blocks: float32 [64, 786432], P(None, ('groups', 'sub')), parts along dimension 1, may hold values from -0.75 to 0.75
- if_rows: int32 [1024], P(('groups', 'sub')), parts along dimension 0, may hold values from 0 to 191
- send_rows: int32 [1024], P(('groups', 'sub')), parts along dimension 0, may hold values from 0 to 191
- if_count: int32 [32], P(('groups', 'sub')), parts along dimension 0, may hold values from 1 to 32, as said below
- if_blocks: float32 [64, 65536], P(None, ('groups', 'sub')), parts along dimension 1, may hold values from -0.75 to 0.75
- coarse_basis: float32 [64, 393216], P(None, ('groups', 'sub')), parts along dimension 1, may hold values from -0.109375 to 0.109375
- coarse_factor: float32 [2048, 1024], P(('groups', 'sub')), parts along dimension 0, may hold values from -0.1875 to 0.1875
Outputs:
- solution: float32 [32, 196608], P('groups', 'sub'), parts along dimension 0
- precond_residual: float32 [32, 196608], P('groups', 'sub'), parts along dimension 0
The draws below stay inside these ranges and needn't reach their ends.
There are 2 independent parts, one for each index of `groups`. The reference program is written for one: setup_inputs(seed, part) draws one part's arguments, and reference() takes and returns one part's arrays. A program takes and returns all parts, laid end to end along the dimension named above; each array names one. Nothing has to cross between parts.
Inputs may be any that keep to these rules, and one draw needn't show every extreme that they name: `local_edges`: the two rows of each element differ. `if_count`: some subdomain has exactly 32 live slots in every draw.
All inputs are finite; a program needn't handle non-finite values.
Results may differ from the reference program's by a relative error of at most 0.0003.
Values sent between devices are 32-bit elements; how exact they have to be, the bound alone decides.
A program may use at most 128 MiB of HBM per device.

```python
import math
import jax
import jax.numpy as jnp
from jax import lax

BS = 64
LOADS = 16
NDEF = 64
NB = 192
IF = 32
ITERS = 2
NE = 384
NC = 1024
DOFS = 196608
N_SUB = 16


def draw_local_edges(key, part):
    key = jax.random.fold_in(key, 11)
    first_key, step_key = jax.random.split(key)
    first = jax.random.randint(first_key, (N_SUB * NE,), 0, NB)
    offset = jax.random.randint(step_key, (N_SUB * NE,), 1, NB)
    second = (first + offset) % NB
    return jnp.stack([first, second]).astype(jnp.int32)


def draw_if_count(key, part):
    key = jax.random.fold_in(key, 12)
    count_key, pick_key = jax.random.split(key)
    counts = jax.random.randint(count_key, (N_SUB,), max(1, IF // 4), IF + 1)
    chosen = jax.random.randint(pick_key, (), 0, N_SUB)
    return counts.at[chosen].set(IF).astype(jnp.int32)


def plant(entries, stream_key, smallest, largest):
    dims = entries.shape
    index_at = [jax.random.randint(jax.random.fold_in(stream_key, axis), (), 0, dims[axis]) for axis in range(len(dims))]
    entries = entries.at[tuple(index_at)].set(smallest)
    longest = dims.index(max(dims))
    index_at[longest] = (index_at[longest] + 1) % dims[longest]
    return entries.at[tuple(index_at)].set(largest)


def block_levels(key, shape, cuts, least, largest):
    gain, own = 1.0, jax.random.fold_in(key, 6)
    for position, blocks in cuts:
        steps = jnp.exp(jax.random.uniform(jax.random.fold_in(own, position), (blocks,), jnp.float32, least / len(cuts), largest / len(cuts)))
        gain = gain * jnp.repeat(steps, shape[position] // blocks).reshape([-1 if axis == position else 1 for axis in range(len(shape))])
    return gain


def gaussian(key, dims, scale, reach, cuts=(), kind=jnp.bfloat16):
    entries = scale * jax.random.normal(key, dims, jnp.float32)
    if cuts:
        entries = entries * block_levels(key, dims, cuts, -0.22, 0.18)
    return jnp.clip(entries, -reach, reach).astype(kind)


def setup_inputs(seed: int = 0, part: int = 0) -> dict:
    key_of = jax.random.split(jax.random.key(seed), 12)
    part_splits = jax.random.split(jax.random.fold_in(key_of[11], part), 12)
    rhs = gaussian(part_splits[0], (LOADS, DOFS), 1.0, 8.0, ((1, 16),), jnp.float32)
    mass = jnp.clip(jnp.exp(math.log(2.0) - 1.3862944 * jax.random.uniform(part_splits[1], (DOFS,), jnp.float32) ** block_levels(part_splits[1], (DOFS,), ((0, 16),), -0.2, 0.2)), 0.5, 2.0)
    jacobi = jnp.clip(jnp.exp(math.log(1.0) - 2.3025851 * jax.random.uniform(part_splits[2], (DOFS,), jnp.float32) ** block_levels(part_splits[2], (DOFS,), ((0, 16),), -0.2, 0.2)), 0.1, 1.0)
    local_edges = draw_local_edges(jax.random.fold_in(jax.random.fold_in(key_of[11], part), 71), part)
    local_blocks = gaussian(part_splits[4], (BS, N_SUB * NE * BS), BS ** -0.5, 0.75, ((1, 16),), jnp.float32)
    if_rows = plant(jax.random.randint(part_splits[5], (N_SUB * IF,), 0, NB), jax.random.fold_in(part_splits[5], 1), 0, NB - 1).astype(jnp.int32)
    send_rows = plant(jax.random.randint(part_splits[6], (N_SUB * IF,), 0, NB), jax.random.fold_in(part_splits[6], 1), 0, NB - 1).astype(jnp.int32)
    if_count = draw_if_count(jax.random.fold_in(jax.random.fold_in(key_of[11], part), 71), part)
    if_blocks = gaussian(part_splits[8], (BS, N_SUB * IF * BS), BS ** -0.5, 0.75, ((1, 16),), jnp.float32)
    coarse_basis = gaussian(part_splits[9], (NDEF, DOFS), (NB * BS // 4) ** -0.5, 0.109375, ((1, 16),), jnp.float32)
    coarse_factor = gaussian(part_splits[10], (NC, NC), NC ** -0.5, 0.1875, ((0, 16),), jnp.float32)
    return dict(rhs=rhs, mass=mass, jacobi=jacobi, local_edges=local_edges, local_blocks=local_blocks, if_rows=if_rows, send_rows=send_rows, if_count=if_count, if_blocks=if_blocks, coarse_basis=coarse_basis, coarse_factor=coarse_factor)


HIGH = lax.Precision.HIGHEST


def one_hot(index, width):
    return (index[:, None] == jnp.arange(width, dtype=jnp.int32)[None, :]).astype(jnp.float32)


def element_force(diff, blocks):
    strain = jnp.einsum('rek,kej->rej', diff, blocks, precision=HIGH)
    return jnp.einsum('rej,kej->rek', strain, blocks, precision=HIGH)


def apply_operator(v, mass, local_edges, local_blocks, if_rows, send_rows, if_count, if_blocks):
    v4 = v.reshape(LOADS, N_SUB, NB, BS)
    edges = local_edges.reshape(2, N_SUB, NE)
    blocks = local_blocks.reshape(BS, N_SUB, NE, BS)
    iface = if_blocks.reshape(BS, N_SUB, IF, BS)
    own = if_rows.reshape(N_SUB, IF)
    sends = send_rows.reshape(N_SUB, IF)
    sends_next = jnp.roll(sends, -1, axis=0)
    neighbour = jnp.roll(v4, -1, axis=1)

    def local_part(vs, first, second, blk):
        force = element_force(vs[:, first] - vs[:, second], blk)
        incidence = one_hot(first, NB) - one_hot(second, NB)
        return jnp.einsum('en,rek->rnk', incidence, force, precision=HIGH)

    local_sum = jax.vmap(local_part, in_axes=(1, 0, 0, 1), out_axes=1)(v4, edges[0], edges[1], blocks)

    def iface_part(vs, vn, own_rows, next_rows, blk, count):
        live = (jnp.arange(IF, dtype=jnp.int32) < count).astype(jnp.float32)
        force = element_force(vs[:, own_rows] - vn[:, next_rows], blk) * live[None, :, None]
        plus = jnp.einsum('en,rek->rnk', one_hot(own_rows, NB), force, precision=HIGH)
        minus = jnp.einsum('en,rek->rnk', one_hot(next_rows, NB), force, precision=HIGH)
        return plus, minus

    plus, minus = jax.vmap(iface_part, in_axes=(1, 1, 0, 0, 1, 0), out_axes=(1, 1))(v4, neighbour, own, sends_next, iface, if_count)
    total = mass.reshape(N_SUB, NB, BS)[None] * v4 + local_sum + plus - jnp.roll(minus, 1, axis=1)
    return total.reshape(LOADS, DOFS)


def precondition(r, jacobi, coarse_basis, coarse_factor):
    r3 = r.reshape(LOADS, N_SUB, NB * BS)
    basis = coarse_basis.reshape(NDEF, N_SUB, NB * BS)
    coarse = jnp.einsum('rsd,ksd->rsk', r3, basis, precision=HIGH).reshape(LOADS, NC)
    whole_w = jnp.dot(coarse, coarse_factor, precision=HIGH)
    back = jnp.dot(whole_w, coarse_factor.T, precision=HIGH).reshape(LOADS, N_SUB, NDEF)
    correction = jnp.einsum('rsk,ksd->rsd', back, basis, precision=HIGH).reshape(LOADS, DOFS)
    return r * jacobi[None, :] + correction


def reference(rhs, mass, jacobi, local_edges, local_blocks, if_rows, send_rows, if_count, if_blocks, coarse_basis, coarse_factor):
    solution = jnp.zeros_like(rhs)
    residual = rhs
    z = precondition(residual, jacobi, coarse_basis, coarse_factor)
    gamma = jnp.sum(residual * z, axis=1)
    direction = z
    for step in range(ITERS):
        image = apply_operator(direction, mass, local_edges, local_blocks, if_rows, send_rows, if_count, if_blocks)
        alpha = gamma / jnp.sum(direction * image, axis=1)
        solution = solution + alpha[:, None] * direction
        residual = residual - alpha[:, None] * image
        z = precondition(residual, jacobi, coarse_basis, coarse_factor)
        if step + 1 < ITERS:
            gamma_next = jnp.sum(residual * z, axis=1)
            direction = z + (gamma_next / gamma)[:, None] * direction
            gamma = gamma_next
    return solution, z
```

```python
import functools

import jax
import jax.numpy as jnp
from jax import lax
from jax.experimental import pallas as pl
from jax.experimental.pallas import tpu as pltpu
from jax.sharding import PartitionSpec as P

ITERS = 2
F32 = jnp.float32
BF16 = jnp.bfloat16
MESH = pl.DeviceIdType.MESH


def split(x):
    high = x.astype(BF16)
    return high, (x - high.astype(F32)).astype(BF16)


def stacked(x):
    high, low = split(x)
    return jnp.concatenate([high, low], axis=0)


def dot(a, b):
    return jnp.dot(a, b, preferred_element_type=F32)


def dot_t(a, b):
    return lax.dot_general(a, b, (((1,), (1,)), ((), ())), preferred_element_type=F32)


def fold(o, rows):
    a = o[:rows] + o[rows:]
    return a + pltpu.roll(a, 64, 1)


def kernel(
    n,
    mass_ref,
    jac_ref,
    edges_s,
    ifr_s,
    snd_s,
    cnt_s,
    edges_v,
    ifr_v,
    snd_v,
    rhs_h,
    blocks_h,
    ifb_h,
    basis_h,
    fac_h,
    x_ref,
    z_ref,
    r_ref,
    p_ref,
    q_ref,
    v_ref,
    qrow_ref,
    t_ref,
    inc_ref,
    stage_ref,
    basis_st,
    fac_st,
    bb_ref,
    bs_ref,
    ff_ref,
    w_ref,
    pw_ref,
    msg_a,
    rcv_a,
    msg_b,
    rcv_b,
    halo_s,
    halo_r,
    frc_s,
    frc_r,
    in_sem,
    sa_sem,
    ra_sem,
    sb_sem,
    rb_sem,
    sh_sem,
    rh_sem,
    sf_sem,
    rf_sem,
):
    loads, width = rhs_h.shape
    rows = width // 64
    ne = edges_v.shape[1]
    slots = ifr_v.shape[1]
    nc = fac_h.shape[1]
    wide_e = t_ref.shape[0] // loads
    me = lax.axis_index("sub")
    nxt = lax.rem(me + 1, n)
    prv = lax.rem(me + n - 1, n)
    lcols = ne * 64

    cp_rhs = pltpu.make_async_copy(rhs_h, r_ref, in_sem.at[0])
    cp_basis = pltpu.make_async_copy(basis_h, basis_st, in_sem.at[1])
    cp_fac = pltpu.make_async_copy(fac_h, fac_st, in_sem.at[2])
    cp_blk = pltpu.make_async_copy(blocks_h, stage_ref.at[:, pl.ds(0, lcols)], in_sem.at[3])
    cp_ifb = pltpu.make_async_copy(ifb_h, stage_ref.at[:, pl.ds(lcols, slots * 64)], in_sem.at[4])
    for cp in (cp_rhs, cp_basis, cp_fac, cp_blk, cp_ifb):
        cp.start()

    barrier = pltpu.get_barrier_semaphore()

    @pl.loop(1, n)
    def _(k):
        pl.semaphore_signal(barrier, inc=1, device_id={"sub": lax.rem(me + k, n)}, device_id_type=MESH)

    low_half = lax.broadcasted_iota(jnp.int32, (loads, 128), 1) < 64
    low_half8 = lax.broadcasted_iota(jnp.int32, (8, 128), 1) < 64
    low_half64 = lax.broadcasted_iota(jnp.int32, (64, 128), 1) < 64
    own_block = (lax.broadcasted_iota(jnp.int32, (64, 256), 0) >> 4) == (lax.broadcasted_iota(jnp.int32, (64, 256), 1) >> 6)

    def lanes(i, size):
        return pl.ds(pl.multiple_of(i * size, size), size)

    def pack16(s):
        return jnp.where(low_half8, s[:8], s[8:])

    def unpack16(t):
        return jnp.concatenate([jnp.broadcast_to(t[:, 0:1], (8, 128)), jnp.broadcast_to(t[:, 64:65], (8, 128))], axis=0)

    def bcast(s):
        return jnp.broadcast_to(jnp.sum(s, axis=1, keepdims=True), (loads, 128))

    def split_into(src, dst, total, size):
        @pl.loop(0, total // size)
        def _(i):
            dst[:, lanes(i, size)] = stacked(src[:, lanes(i, size)])

    def contract(src, mat, total, size):
        def step(i, o):
            return o + dot_t(stacked(src[:, lanes(i, size)]), mat[:, lanes(i, size)])
        o = lax.fori_loop(0, total // size, step, jnp.zeros((2 * loads, 128), F32))
        return fold(o, loads)

    def send_parts(phase, coarse, scalars):
        lhs = stacked(coarse)

        @pl.loop(0, nc // 512)
        def _(i):
            o = dot(lhs, ff_ref[:, lanes(i, 512)])
            o = o[:loads] + o[loads:]
            for c in range(4):
                for h in range(2):
                    msg_a[phase, 8 * i + 2 * c + h, 0:8] = o[8 * h : 8 * h + 8, 128 * c : 128 * c + 128]
                    msg_a[phase, 8 * i + 2 * c + h, 8:16] = scalars

        rcv_a[phase, me] = msg_a[phase, me]

        @pl.loop(1, n)
        def _(k):
            to = lax.rem(me + k, n)
            pltpu.make_async_remote_copy(
                msg_a.at[phase, to], rcv_a.at[phase, me], sa_sem.at[phase], ra_sem.at[phase],
                device_id={"sub": to}, device_id_type=MESH,
            ).start()

    def wait_all(buf, phase, sem):
        part = buf.at[phase, pl.ds(0, n - 1)]
        pltpu.make_async_copy(part, part, sem.at[phase]).wait()

    def take_parts(phase):
        wait_all(rcv_a, phase, ra_sem)
        s = lax.fori_loop(0, n, lambda j, s: s + rcv_a[phase, j], jnp.zeros((16, 128), F32))
        return s[:8], unpack16(s[8:])

    def send_whole(phase, tile, scalars):
        both = jnp.concatenate([tile, scalars], axis=0)
        msg_b[phase] = both
        rcv_b[phase, me] = both

        @pl.loop(1, n)
        def _(k):
            to = lax.rem(me + k, n)
            pltpu.make_async_remote_copy(
                msg_b.at[phase], rcv_b.at[phase, me], sb_sem.at[phase], rb_sem.at[phase],
                device_id={"sub": to}, device_id_type=MESH,
            ).start()

    def take_whole(phase, alpha):
        wait_all(rcv_b, phase, rb_sem)

        def step(m, carry):
            norm, s = carry
            first = rcv_b[phase, 2 * m]
            second = rcv_b[phase, 2 * m + 1]
            w = jnp.concatenate([first[:8], second[:8]], axis=0)
            if alpha is not None:
                w = w_ref[:, lanes(m, 128)] - alpha * w
            w_ref[:, lanes(m, 128)] = w
            return norm + w * w, s + first[8:] + second[8:]

        norm, s = lax.fori_loop(0, n // 2, step, (jnp.zeros((loads, 128), F32), jnp.zeros((8, 128), F32)))
        return bcast(norm) + unpack16(s)

    def weighted(scale_ref, src):
        def step(i, s):
            v = src[:, lanes(i, 512)]
            v = scale_ref[:, lanes(i, 512)] * v * v
            return s + v[:, :128] + v[:, 128:256] + v[:, 256:384] + v[:, 384:]
        return lax.fori_loop(0, width // 512, step, jnp.zeros((loads, 128), F32))

    def precondition(visit):
        lhs = stacked(contract(w_ref, ff_ref, nc, 512))

        @pl.loop(0, width // 512)
        def _(i):
            o = dot(lhs, bs_ref[:, lanes(i, 512)])
            visit(i, jac_ref[:, lanes(i, 512)] * r_ref[:, lanes(i, 512)] + o[:loads] + o[loads:])

    def set_direction(i, p):
        p_ref[:, lanes(i, 512)] = p
        for c in range(4):
            a = p[:, 128 * c : 128 * c + 128]
            b = pltpu.roll(a, 64, 1)
            v_ref[8 * i + 2 * c] = jnp.where(low_half, a, b)
            v_ref[8 * i + 2 * c + 1] = jnp.where(low_half, b, a)

    def put_force(row, t):
        high = t.astype(BF16).astype(F32)
        t_ref[pl.ds(pl.multiple_of(row * loads, 16), t.shape[0]), :] = jnp.where(
            low_half64 if t.shape[0] == 64 else low_half, high, t - high
        )

    def force(d, col):
        b = bb_ref[:, pl.ds(pl.multiple_of(col, 256), 256)]
        u = dot(stacked(d), b)
        u = jnp.where(own_block, u[:64] + u[64:], 0.0)
        t = fold(dot_t(stacked(u), b), 64)
        u2 = u * u
        return t, u2[0:16] + u2[16:32] + u2[32:48] + u2[48:64]

    def local_groups(start, stop, acc):
        def step(g, acc):
            d = jnp.concatenate([v_ref[edges_s[0, 4 * g + k]] - v_ref[edges_s[1, 4 * g + k]] for k in range(4)], axis=0)
            t, e = force(d, 256 * g)
            put_force(4 * g, t)
            return acc + e
        return lax.fori_loop(start, stop, step, acc)

    cp_rhs.wait()
    cp_basis.wait()
    split_into(basis_st, bs_ref, width, 512)
    coarse = contract(r_ref, bs_ref, width, 512)
    cp_fac.wait()
    split_into(fac_st, ff_ref, nc, 512)
    pl.semaphore_wait(barrier, n - 1)
    send_parts(0, coarse, jnp.zeros((8, 128), F32))

    jr2 = bcast(weighted(jac_ref, r_ref))
    row_id = lax.broadcasted_iota(jnp.int32, (rows, ne), 0)
    inc_ref[...] = jnp.zeros_like(inc_ref)
    inc_ref[:, 0:ne] = ((row_id == edges_v[0:1, :]).astype(F32) - (row_id == edges_v[1:2, :]).astype(F32)).astype(BF16)
    row_id = lax.broadcasted_iota(jnp.int32, (rows, slots), 0)
    inc_ref[:, ne : ne + slots] = (row_id == ifr_v[...]).astype(F32).astype(BF16)
    inc_ref[:, ne + slots : ne + 2 * slots] = (-(row_id == snd_v[...]).astype(F32)).astype(BF16)
    used = (ne + 2 * slots) * loads
    if wide_e * loads > used:
        t_ref[used:, :] = jnp.zeros((wide_e * loads - used, 128), F32)

    tile, _ = take_parts(0)
    send_whole(0, tile, pack16(jr2))
    cp_blk.wait()
    cp_ifb.wait()
    split_into(stage_ref, bb_ref, stage_ref.shape[1], 512)
    gamma = take_whole(0, None)
    precondition(set_direction)

    for it in range(ITERS):
        @pl.loop(0, slots // 2)
        def _(k):
            halo_s[it, pl.ds(pl.multiple_of(k * 16, 16), 16), :] = jnp.where(
                low_half, v_ref[snd_s[0, 2 * k]], v_ref[snd_s[0, 2 * k + 1]]
            )

        cp_halo = pltpu.make_async_remote_copy(
            halo_s.at[it], halo_r.at[it], sh_sem.at[it], rh_sem.at[it], device_id={"sub": prv}, device_id_type=MESH
        )
        cp_halo.start()
        half = ne // 8
        acc = local_groups(0, half, jnp.zeros((loads, 256), F32))
        cp_halo.wait()

        def iface(g, acc):
            parts = []
            for a in range(2):
                x = halo_r[it, pl.ds(pl.multiple_of((2 * g + a) * 16, 16), 16), :]
                y = pltpu.roll(x, 64, 1)
                for b, there in enumerate((jnp.where(low_half, x, y), jnp.where(low_half, y, x))):
                    k = 4 * g + 2 * a + b
                    live = jnp.where(k < cnt_s[0], 1.0, 0.0).astype(F32)
                    parts.append((v_ref[ifr_s[0, k]] - there) * live)
            t, e = force(jnp.concatenate(parts, axis=0), lcols + 256 * g)
            put_force(ne + 4 * g, t)
            for a in range(2):
                frc_s[it, pl.ds(pl.multiple_of((2 * g + a) * 16, 16), 16), :] = jnp.where(
                    low_half, t[32 * a : 32 * a + 16], t[32 * a + 16 : 32 * a + 32]
                )
            return acc + e

        acc = lax.fori_loop(0, slots // 4, iface, acc)
        cp_frc = pltpu.make_async_remote_copy(
            frc_s.at[it], frc_r.at[it], sf_sem.at[it], rf_sem.at[it], device_id={"sub": nxt}, device_id_type=MESH
        )
        cp_frc.start()
        acc = local_groups(half, ne // 4, acc)
        energy = weighted(mass_ref, p_ref) + acc[:, :128] + acc[:, 128:]
        cp_frc.wait()

        @pl.loop(0, slots // 2)
        def _(k):
            x = frc_r[it, pl.ds(pl.multiple_of(k * 16, 16), 16), :]
            y = pltpu.roll(x, 64, 1)
            put_force(ne + slots + 2 * k, jnp.where(low_half, x, y))
            put_force(ne + slots + 2 * k + 1, jnp.where(low_half, y, x))

        @pl.loop(0, loads // 2)
        def _(k):
            f = jnp.concatenate([t_ref[pl.ds(2 * k + h, wide_e, stride=loads), :] for h in range(2)], axis=1).astype(BF16)
            o = dot(inc_ref[...], f)
            for h in range(2):
                a = o[:, 128 * h : 128 * h + 128]
                qrow_ref[pl.ds(2 * k + h, rows, stride=loads), :] = a + pltpu.roll(a, 64, 1)

        def image(i, o):
            cols = []
            for c in range(4):
                pair = qrow_ref[pl.ds(pl.multiple_of((8 * i + 2 * c) * 16, 32), 32), :]
                cols.append(jnp.where(low_half, pair[:16], pair[16:]))
            q = mass_ref[:, lanes(i, 512)] * p_ref[:, lanes(i, 512)] + jnp.concatenate(cols, axis=1)
            q_ref[:, lanes(i, 512)] = q
            return o + dot_t(stacked(q), bs_ref[:, lanes(i, 512)])

        coarse = fold(lax.fori_loop(0, width // 512, image, jnp.zeros((2 * loads, 128), F32)), loads)
        send_parts(it + 1, coarse, pack16(bcast(energy)))
        tile, energy = take_parts(it + 1)
        alpha = gamma / energy
        alpha4 = jnp.concatenate([alpha] * 4, axis=1)

        def update(i, s):
            r = r_ref[:, lanes(i, 512)] - alpha4 * q_ref[:, lanes(i, 512)]
            r_ref[:, lanes(i, 512)] = r
            v = jac_ref[:, lanes(i, 512)] * r * r
            return s + v[:, :128] + v[:, 128:256] + v[:, 256:384] + v[:, 384:]

        jr2 = bcast(lax.fori_loop(0, width // 512, update, jnp.zeros((loads, 128), F32)))
        send_whole(it + 1, tile, pack16(jr2))

        @pl.loop(0, width // 512)
        def _(i):
            step = alpha4 * p_ref[:, lanes(i, 512)]
            x_ref[:, lanes(i, 512)] = step if it == 0 else x_ref[:, lanes(i, 512)] + step

        new = take_whole(it + 1, alpha)
        if it + 1 < ITERS:
            beta4 = jnp.concatenate([new / gamma] * 4, axis=1)
            precondition(lambda i, z: set_direction(i, z + beta4 * p_ref[:, lanes(i, 512)]))
            gamma = new
        else:
            def finish(i, z):
                z_ref[:, lanes(i, 512)] = z
            precondition(finish)

    for phase in range(ITERS + 1):
        wait_all(rcv_a, phase, sa_sem)
        wait_all(rcv_b, phase, sb_sem)


def body(
    rhs,
    mass,
    jacobi,
    local_edges,
    local_blocks,
    if_rows,
    send_rows,
    if_count,
    if_blocks,
    coarse_basis,
    coarse_factor,
):
    n = lax.axis_size("sub")
    loads, width = rhs.shape
    ne = local_edges.shape[1]
    slots = if_rows.shape[0]
    nc = coarse_factor.shape[1]
    rows = width // 64
    wide_e = -(-(ne + 2 * slots) // 128) * 128
    cols = (ne + slots) * 64
    phases = ITERS + 1
    vmem = pl.BlockSpec(memory_space=pltpu.VMEM)
    smem = pl.BlockSpec(memory_space=pltpu.SMEM)
    hbm = pl.BlockSpec(memory_space=pl.ANY)
    dma = pltpu.SemaphoreType.DMA
    if_rows = if_rows.reshape(1, slots)
    send_rows = send_rows.reshape(1, slots)
    out = jax.ShapeDtypeStruct((loads, width), F32)
    return pl.pallas_call(
        functools.partial(kernel, n),
        out_shape=(out, out),
        in_specs=[vmem] * 2 + [smem] * 4 + [vmem] * 3 + [hbm] * 5,
        out_specs=(vmem, vmem),
        scratch_shapes=[
            pltpu.VMEM((loads, width), F32),
            pltpu.VMEM((loads, width), F32),
            pltpu.VMEM((loads, width), F32),
            pltpu.VMEM((rows, loads, 128), F32),
            pltpu.VMEM((rows * loads, 128), F32),
            pltpu.VMEM((wide_e * loads, 128), F32),
            pltpu.VMEM((rows, wide_e), BF16),
            pltpu.VMEM((64, cols), F32),
            pltpu.VMEM((64, width), F32),
            pltpu.VMEM((64, nc), F32),
            pltpu.VMEM((128, cols), BF16),
            pltpu.VMEM((128, width), BF16),
            pltpu.VMEM((128, nc), BF16),
            pltpu.VMEM((loads, nc), F32),
            pltpu.VMEM((8, 128), F32),
            pltpu.VMEM((phases, n, 16, 128), F32),
            pltpu.VMEM((phases, n, 16, 128), F32),
            pltpu.VMEM((phases, 16, 128), F32),
            pltpu.VMEM((phases, n, 16, 128), F32),
            pltpu.VMEM((ITERS, slots * 8, 128), F32),
            pltpu.VMEM((ITERS, slots * 8, 128), F32),
            pltpu.VMEM((ITERS, slots * 8, 128), F32),
            pltpu.VMEM((ITERS, slots * 8, 128), F32),
            dma((5,)),
            dma((phases,)),
            dma((phases,)),
            dma((phases,)),
            dma((phases,)),
            dma((ITERS,)),
            dma((ITERS,)),
            dma((ITERS,)),
            dma((ITERS,)),
        ],
        compiler_params=pltpu.CompilerParams(collective_id=0, has_side_effects=True, vmem_limit_bytes=56 * 2**20),
    )(
        mass.reshape(1, width),
        jacobi.reshape(1, width),
        local_edges,
        if_rows,
        send_rows,
        if_count,
        local_edges,
        if_rows,
        send_rows,
        rhs,
        local_blocks,
        if_blocks,
        coarse_basis,
        coarse_factor,
    )


def solution(mesh):
    in_specs = (
        P("groups", "sub"),
        P(("groups", "sub")),
        P(("groups", "sub")),
        P(None, ("groups", "sub")),
        P(None, ("groups", "sub")),
        P(("groups", "sub")),
        P(("groups", "sub")),
        P(("groups", "sub")),
        P(None, ("groups", "sub")),
        P(None, ("groups", "sub")),
        P(("groups", "sub"), None),
    )
    out_specs = (P("groups", "sub"), P("groups", "sub"))
    return jax.shard_map(body, mesh=mesh, in_specs=in_specs, out_specs=out_specs, check_vma=False)
```

```python
import functools

import jax
import jax.numpy as jnp
from jax import lax
from jax.experimental import pallas as pl
from jax.experimental.pallas import tpu as pltpu
from jax.sharding import PartitionSpec as P

ITERS = 2
F32 = jnp.float32
BF16 = jnp.bfloat16
MESH = pl.DeviceIdType.MESH
GROUPS = 8
UNROLL = 4


def split(x):
    high = x.astype(BF16)
    return high, (x - high.astype(F32)).astype(BF16)


def stacked(x):
    high, low = split(x)
    return jnp.concatenate([high, low], axis=0)


def dot(a, b):
    return jnp.dot(a, b, preferred_element_type=F32)


def dot_t(a, b):
    return lax.dot_general(a, b, (((1,), (1,)), ((), ())), preferred_element_type=F32)


def fold(o, rows):
    a = o[:rows] + o[rows:]
    return a + pltpu.roll(a, 64, 1)


def kernel(
    n,
    mass_ref,
    jac_ref,
    edges_s,
    ifr_s,
    snd_s,
    cnt_s,
    edges_v,
    ifr_v,
    snd_v,
    rhs_h,
    blocks_h,
    ifb_h,
    basis_h,
    fac_h,
    x_ref,
    z_ref,
    r_ref,
    p_ref,
    q_ref,
    v_ref,
    qrow_ref,
    t_ref,
    inc_ref,
    stage_ref,
    basis_st,
    fac_st,
    bb_ref,
    bs_ref,
    ff_ref,
    w_ref,
    pw_ref,
    msg_a,
    rcv_a,
    msg_b,
    rcv_b,
    halo_s,
    halo_r,
    frc_s,
    frc_r,
    in_sem,
    sa_sem,
    ra_sem,
    sb_sem,
    rb_sem,
    sh_sem,
    rh_sem,
    sf_sem,
    rf_sem,
):
    loads, width = rhs_h.shape
    rows = width // 64
    ne = edges_v.shape[1]
    slots = ifr_v.shape[1]
    nc = fac_h.shape[1]
    wide_e = t_ref.shape[0] // loads
    me = lax.axis_index("sub")
    nxt = lax.rem(me + 1, n)
    prv = lax.rem(me + n - 1, n)
    lcols = ne * 64

    cp_rhs = pltpu.make_async_copy(rhs_h, r_ref, in_sem.at[0])
    cp_basis = pltpu.make_async_copy(basis_h, basis_st, in_sem.at[1])
    cp_fac = pltpu.make_async_copy(fac_h, fac_st, in_sem.at[2])
    cp_blk = pltpu.make_async_copy(blocks_h, stage_ref.at[:, pl.ds(0, lcols)], in_sem.at[3])
    cp_ifb = pltpu.make_async_copy(ifb_h, stage_ref.at[:, pl.ds(lcols, slots * 64)], in_sem.at[4])
    for cp in (cp_rhs, cp_basis, cp_fac, cp_blk, cp_ifb):
        cp.start()

    barrier = pltpu.get_barrier_semaphore()

    @pl.loop(1, n)
    def _(k):
        pl.semaphore_signal(barrier, inc=1, device_id={"sub": lax.rem(me + k, n)}, device_id_type=MESH)

    low_half = lax.broadcasted_iota(jnp.int32, (loads, 128), 1) < 64
    low_half8 = lax.broadcasted_iota(jnp.int32, (8, 128), 1) < 64
    low_half64 = lax.broadcasted_iota(jnp.int32, (64, 128), 1) < 64
    own_block = (lax.broadcasted_iota(jnp.int32, (64, 256), 0) >> 4) == (lax.broadcasted_iota(jnp.int32, (64, 256), 1) >> 6)

    def lanes(i, size):
        return pl.ds(pl.multiple_of(i * size, size), size)

    def pack16(s):
        return jnp.where(low_half8, s[:8], s[8:])

    def unpack16(t):
        return jnp.concatenate([jnp.broadcast_to(t[:, 0:1], (8, 128)), jnp.broadcast_to(t[:, 64:65], (8, 128))], axis=0)

    def bcast(s):
        return jnp.broadcast_to(jnp.sum(s, axis=1, keepdims=True), (loads, 128))

    def split_into(src, dst, total, size):
        @pl.loop(0, total // size, unroll=2)
        def _(i):
            dst[:, lanes(i, size)] = stacked(src[:, lanes(i, size)])

    def contract(src, mat, total, size):
        def step(i, o):
            return o + dot_t(stacked(src[:, lanes(i, size)]), mat[:, lanes(i, size)])
        o = lax.fori_loop(0, total // size, step, jnp.zeros((2 * loads, 128), F32), unroll=2)
        return fold(o, loads)

    def send_parts(phase, coarse, scalars):
        lhs = stacked(coarse)

        @pl.loop(0, nc // 512, unroll=2)
        def _(i):
            o = dot(lhs, ff_ref[:, lanes(i, 512)])
            o = o[:loads] + o[loads:]
            for c in range(4):
                for h in range(2):
                    msg_a[phase, 8 * i + 2 * c + h, 0:8] = o[8 * h : 8 * h + 8, 128 * c : 128 * c + 128]
                    msg_a[phase, 8 * i + 2 * c + h, 8:16] = scalars

        rcv_a[phase, me] = msg_a[phase, me]

        @pl.loop(1, n)
        def _(k):
            to = lax.rem(me + k, n)
            pltpu.make_async_remote_copy(
                msg_a.at[phase, to], rcv_a.at[phase, me], sa_sem.at[phase], ra_sem.at[phase],
                device_id={"sub": to}, device_id_type=MESH,
            ).start()

    def wait_all(buf, phase, sem):
        part = buf.at[phase, pl.ds(0, n - 1)]
        pltpu.make_async_copy(part, part, sem.at[phase]).wait()

    def take_parts(phase):
        wait_all(rcv_a, phase, ra_sem)
        s = lax.fori_loop(0, n, lambda j, s: s + rcv_a[phase, j], jnp.zeros((16, 128), F32), unroll=8)
        return s[:8], unpack16(s[8:])

    def send_whole(phase, tile, scalars):
        both = jnp.concatenate([tile, scalars], axis=0)
        msg_b[phase] = both
        rcv_b[phase, me] = both

        @pl.loop(1, n)
        def _(k):
            to = lax.rem(me + k, n)
            pltpu.make_async_remote_copy(
                msg_b.at[phase], rcv_b.at[phase, me], sb_sem.at[phase], rb_sem.at[phase],
                device_id={"sub": to}, device_id_type=MESH,
            ).start()

    def take_whole(phase, alpha):
        wait_all(rcv_b, phase, rb_sem)

        def step(m, carry):
            norm, s = carry
            first = rcv_b[phase, 2 * m]
            second = rcv_b[phase, 2 * m + 1]
            w = jnp.concatenate([first[:8], second[:8]], axis=0)
            if alpha is not None:
                w = w_ref[:, lanes(m, 128)] - alpha * w
            w_ref[:, lanes(m, 128)] = w
            return norm + w * w, s + first[8:] + second[8:]

        norm, s = lax.fori_loop(0, n // 2, step, (jnp.zeros((loads, 128), F32), jnp.zeros((8, 128), F32)), unroll=4)
        return bcast(norm) + unpack16(s)

    def weighted(scale_ref, src):
        def step(i, s):
            v = src[:, lanes(i, 512)]
            v = scale_ref[:, lanes(i, 512)] * v * v
            return s + v[:, :128] + v[:, 128:256] + v[:, 256:384] + v[:, 384:]
        return lax.fori_loop(0, width // 512, step, jnp.zeros((loads, 128), F32), unroll=UNROLL)

    def precondition(visit):
        lhs = stacked(contract(w_ref, ff_ref, nc, 512))

        @pl.loop(0, width // 512, unroll=UNROLL)
        def _(i):
            o = dot(lhs, bs_ref[:, lanes(i, 512)])
            visit(i, jac_ref[:, lanes(i, 512)] * r_ref[:, lanes(i, 512)] + o[:loads] + o[loads:])

    def set_direction(i, p):
        p_ref[:, lanes(i, 512)] = p
        for c in range(4):
            a = p[:, 128 * c : 128 * c + 128]
            b = pltpu.roll(a, 64, 1)
            v_ref[8 * i + 2 * c] = jnp.where(low_half, a, b)
            v_ref[8 * i + 2 * c + 1] = jnp.where(low_half, b, a)

    def put_force(row, t):
        high = t.astype(BF16).astype(F32)
        t_ref[pl.ds(pl.multiple_of(row * loads, 16), t.shape[0]), :] = jnp.where(
            low_half64 if t.shape[0] == 64 else low_half, high, t - high
        )

    def force(diffs, cols):
        mats = [bb_ref[:, pl.ds(pl.multiple_of(col, 256), 256)] for col in cols]
        strains = [dot(stacked(d), b) for d, b in zip(diffs, mats)]
        strains = [jnp.where(own_block, u[:64] + u[64:], 0.0) for u in strains]
        forces = [fold(dot_t(stacked(u), b), 64) for u, b in zip(strains, mats)]
        squares = [u * u for u in strains]
        return forces, [u[0:16] + u[16:32] + u[32:48] + u[48:64] for u in squares]

    def local_groups(start, stop, acc):
        def step(i, acc):
            groups = [GROUPS * i + b for b in range(GROUPS)]
            diffs = []
            for g in groups:
                rows = [v_ref[edges_s[0, 4 * g + k]] - v_ref[edges_s[1, 4 * g + k]] for k in range(4)]
                diffs.append(jnp.concatenate(rows, axis=0))
            forces, energies = force(diffs, [256 * g for g in groups])
            for g, t in zip(groups, forces):
                put_force(4 * g, t)
            return acc + sum(energies)
        return lax.fori_loop(start // GROUPS, stop // GROUPS, step, acc)

    cp_rhs.wait()
    cp_basis.wait()
    split_into(basis_st, bs_ref, width, 512)
    coarse = contract(r_ref, bs_ref, width, 512)
    cp_fac.wait()
    split_into(fac_st, ff_ref, nc, 512)
    pl.semaphore_wait(barrier, n - 1)
    send_parts(0, coarse, jnp.zeros((8, 128), F32))

    jr2 = bcast(weighted(jac_ref, r_ref))
    row_id = lax.broadcasted_iota(jnp.int32, (rows, ne), 0)
    inc_ref[...] = jnp.zeros_like(inc_ref)
    inc_ref[:, 0:ne] = ((row_id == edges_v[0:1, :]).astype(F32) - (row_id == edges_v[1:2, :]).astype(F32)).astype(BF16)
    row_id = lax.broadcasted_iota(jnp.int32, (rows, slots), 0)
    inc_ref[:, ne : ne + slots] = (row_id == ifr_v[...]).astype(F32).astype(BF16)
    inc_ref[:, ne + slots : ne + 2 * slots] = (-(row_id == snd_v[...]).astype(F32)).astype(BF16)
    used = (ne + 2 * slots) * loads
    if wide_e * loads > used:
        t_ref[used:, :] = jnp.zeros((wide_e * loads - used, 128), F32)

    tile, _ = take_parts(0)
    send_whole(0, tile, pack16(jr2))
    cp_blk.wait()
    cp_ifb.wait()
    split_into(stage_ref, bb_ref, stage_ref.shape[1], 512)
    gamma = take_whole(0, None)
    precondition(set_direction)

    for it in range(ITERS):
        @pl.loop(0, slots // 2, unroll=UNROLL)
        def _(k):
            halo_s[it, pl.ds(pl.multiple_of(k * 16, 16), 16), :] = jnp.where(
                low_half, v_ref[snd_s[0, 2 * k]], v_ref[snd_s[0, 2 * k + 1]]
            )

        cp_halo = pltpu.make_async_remote_copy(
            halo_s.at[it], halo_r.at[it], sh_sem.at[it], rh_sem.at[it], device_id={"sub": prv}, device_id_type=MESH
        )
        cp_halo.start()
        half = ne // 8
        acc = local_groups(0, half, jnp.zeros((loads, 256), F32))
        cp_halo.wait()

        def iface(g, acc):
            parts = []
            for a in range(2):
                x = halo_r[it, pl.ds(pl.multiple_of((2 * g + a) * 16, 16), 16), :]
                y = pltpu.roll(x, 64, 1)
                for b, there in enumerate((jnp.where(low_half, x, y), jnp.where(low_half, y, x))):
                    k = 4 * g + 2 * a + b
                    live = jnp.where(k < cnt_s[0], 1.0, 0.0).astype(F32)
                    parts.append((v_ref[ifr_s[0, k]] - there) * live)
            (t,), (e,) = force([jnp.concatenate(parts, axis=0)], [lcols + 256 * g])
            put_force(ne + 4 * g, t)
            for a in range(2):
                frc_s[it, pl.ds(pl.multiple_of((2 * g + a) * 16, 16), 16), :] = jnp.where(
                    low_half, t[32 * a : 32 * a + 16], t[32 * a + 16 : 32 * a + 32]
                )
            return acc + e

        acc = lax.fori_loop(0, slots // 4, iface, acc, unroll=4)
        cp_frc = pltpu.make_async_remote_copy(
            frc_s.at[it], frc_r.at[it], sf_sem.at[it], rf_sem.at[it], device_id={"sub": nxt}, device_id_type=MESH
        )
        cp_frc.start()
        acc = local_groups(half, ne // 4, acc)
        energy = weighted(mass_ref, p_ref) + acc[:, :128] + acc[:, 128:]
        cp_frc.wait()

        @pl.loop(0, slots // 2, unroll=UNROLL)
        def _(k):
            x = frc_r[it, pl.ds(pl.multiple_of(k * 16, 16), 16), :]
            y = pltpu.roll(x, 64, 1)
            put_force(ne + slots + 2 * k, jnp.where(low_half, x, y))
            put_force(ne + slots + 2 * k + 1, jnp.where(low_half, y, x))

        @pl.loop(0, loads // 2, unroll=2)
        def _(k):
            f = jnp.concatenate([t_ref[pl.ds(2 * k + h, wide_e, stride=loads), :] for h in range(2)], axis=1).astype(BF16)
            o = dot(inc_ref[...], f)
            for h in range(2):
                a = o[:, 128 * h : 128 * h + 128]
                qrow_ref[pl.ds(2 * k + h, rows, stride=loads), :] = a + pltpu.roll(a, 64, 1)

        def image(i, o):
            cols = []
            for c in range(4):
                pair = qrow_ref[pl.ds(pl.multiple_of((8 * i + 2 * c) * 16, 32), 32), :]
                cols.append(jnp.where(low_half, pair[:16], pair[16:]))
            q = mass_ref[:, lanes(i, 512)] * p_ref[:, lanes(i, 512)] + jnp.concatenate(cols, axis=1)
            q_ref[:, lanes(i, 512)] = q
            return o + dot_t(stacked(q), bs_ref[:, lanes(i, 512)])

        coarse = fold(lax.fori_loop(0, width // 512, image, jnp.zeros((2 * loads, 128), F32), unroll=UNROLL), loads)
        send_parts(it + 1, coarse, pack16(bcast(energy)))
        tile, energy = take_parts(it + 1)
        alpha = gamma / energy
        alpha4 = jnp.concatenate([alpha] * 4, axis=1)

        def update(i, s):
            r = r_ref[:, lanes(i, 512)] - alpha4 * q_ref[:, lanes(i, 512)]
            r_ref[:, lanes(i, 512)] = r
            v = jac_ref[:, lanes(i, 512)] * r * r
            return s + v[:, :128] + v[:, 128:256] + v[:, 256:384] + v[:, 384:]

        jr2 = bcast(lax.fori_loop(0, width // 512, update, jnp.zeros((loads, 128), F32), unroll=UNROLL))
        send_whole(it + 1, tile, pack16(jr2))

        @pl.loop(0, width // 512, unroll=UNROLL)
        def _(i):
            step = alpha4 * p_ref[:, lanes(i, 512)]
            x_ref[:, lanes(i, 512)] = step if it == 0 else x_ref[:, lanes(i, 512)] + step

        new = take_whole(it + 1, alpha)
        if it + 1 < ITERS:
            beta4 = jnp.concatenate([new / gamma] * 4, axis=1)
            precondition(lambda i, z: set_direction(i, z + beta4 * p_ref[:, lanes(i, 512)]))
            gamma = new
        else:
            def finish(i, z):
                z_ref[:, lanes(i, 512)] = z
            precondition(finish)

    for phase in range(ITERS + 1):
        wait_all(rcv_a, phase, sa_sem)
        wait_all(rcv_b, phase, sb_sem)


def body(
    rhs,
    mass,
    jacobi,
    local_edges,
    local_blocks,
    if_rows,
    send_rows,
    if_count,
    if_blocks,
    coarse_basis,
    coarse_factor,
):
    n = lax.axis_size("sub")
    loads, width = rhs.shape
    ne = local_edges.shape[1]
    slots = if_rows.shape[0]
    nc = coarse_factor.shape[1]
    rows = width // 64
    wide_e = -(-(ne + 2 * slots) // 128) * 128
    cols = (ne + slots) * 64
    phases = ITERS + 1
    vmem = pl.BlockSpec(memory_space=pltpu.VMEM)
    smem = pl.BlockSpec(memory_space=pltpu.SMEM)
    hbm = pl.BlockSpec(memory_space=pl.ANY)
    dma = pltpu.SemaphoreType.DMA
    if_rows = if_rows.reshape(1, slots)
    send_rows = send_rows.reshape(1, slots)
    out = jax.ShapeDtypeStruct((loads, width), F32)
    return pl.pallas_call(
        functools.partial(kernel, n),
        out_shape=(out, out),
        in_specs=[vmem] * 2 + [smem] * 4 + [vmem] * 3 + [hbm] * 5,
        out_specs=(vmem, vmem),
        scratch_shapes=[
            pltpu.VMEM((loads, width), F32),
            pltpu.VMEM((loads, width), F32),
            pltpu.VMEM((loads, width), F32),
            pltpu.VMEM((rows, loads, 128), F32),
            pltpu.VMEM((rows * loads, 128), F32),
            pltpu.VMEM((wide_e * loads, 128), F32),
            pltpu.VMEM((rows, wide_e), BF16),
            pltpu.VMEM((64, cols), F32),
            pltpu.VMEM((64, width), F32),
            pltpu.VMEM((64, nc), F32),
            pltpu.VMEM((128, cols), BF16),
            pltpu.VMEM((128, width), BF16),
            pltpu.VMEM((128, nc), BF16),
            pltpu.VMEM((loads, nc), F32),
            pltpu.VMEM((8, 128), F32),
            pltpu.VMEM((phases, n, 16, 128), F32),
            pltpu.VMEM((phases, n, 16, 128), F32),
            pltpu.VMEM((phases, 16, 128), F32),
            pltpu.VMEM((phases, n, 16, 128), F32),
            pltpu.VMEM((ITERS, slots * 8, 128), F32),
            pltpu.VMEM((ITERS, slots * 8, 128), F32),
            pltpu.VMEM((ITERS, slots * 8, 128), F32),
            pltpu.VMEM((ITERS, slots * 8, 128), F32),
            dma((5,)),
            dma((phases,)),
            dma((phases,)),
            dma((phases,)),
            dma((phases,)),
            dma((ITERS,)),
            dma((ITERS,)),
            dma((ITERS,)),
            dma((ITERS,)),
        ],
        compiler_params=pltpu.CompilerParams(collective_id=0, has_side_effects=True, vmem_limit_bytes=56 * 2**20),
    )(
        mass.reshape(1, width),
        jacobi.reshape(1, width),
        local_edges,
        if_rows,
        send_rows,
        if_count,
        local_edges,
        if_rows,
        send_rows,
        rhs,
        local_blocks,
        if_blocks,
        coarse_basis,
        coarse_factor,
    )


def solution(mesh):
    in_specs = (
        P("groups", "sub"),
        P(("groups", "sub")),
        P(("groups", "sub")),
        P(None, ("groups", "sub")),
        P(None, ("groups", "sub")),
        P(("groups", "sub")),
        P(("groups", "sub")),
        P(("groups", "sub")),
        P(None, ("groups", "sub")),
        P(None, ("groups", "sub")),
        P(("groups", "sub"), None),
    )
    out_specs = (P("groups", "sub"), P("groups", "sub"))
    return jax.shard_map(body, mesh=mesh, in_specs=in_specs, out_specs=out_specs, check_vma=False)
```

```python
import functools

import jax
import jax.numpy as jnp
from jax import lax
from jax.experimental import pallas as pl
from jax.experimental.pallas import tpu as pltpu
from jax.sharding import PartitionSpec as P

ITERS = 2
F32 = jnp.float32
BF16 = jnp.bfloat16
MESH = pl.DeviceIdType.MESH
GROUPS = 8
PIECES = 4
UNROLL = 4


def split(x):
    high = x.astype(BF16)
    return high, (x - high.astype(F32)).astype(BF16)


def stacked(x):
    high, low = split(x)
    return jnp.concatenate([high, low], axis=0)


def dot(a, b):
    return jnp.dot(a, b, preferred_element_type=F32)


def dot_t(a, b):
    return lax.dot_general(a, b, (((1,), (1,)), ((), ())), preferred_element_type=F32)


def fold(o, rows):
    a = o[:rows] + o[rows:]
    return a + pltpu.roll(a, 64, 1)


def kernel(
    n,
    mass_ref,
    jac_ref,
    edges_s,
    ifr_s,
    snd_s,
    cnt_s,
    edges_v,
    ifr_v,
    snd_v,
    rhs_h,
    blocks_h,
    ifb_h,
    basis_h,
    fac_h,
    x_ref,
    z_ref,
    r_ref,
    p_ref,
    q_ref,
    v_ref,
    qrow_ref,
    t_ref,
    inc_ref,
    stage_ref,
    basis_st,
    fac_st,
    bb_ref,
    bs_ref,
    ff_ref,
    w_ref,
    msg_a,
    rcv_a,
    msg_b,
    rcv_b,
    msg_c,
    rcv_c,
    halo_s,
    halo_r,
    frc_s,
    frc_r,
    in_sem,
    sa_sem,
    ra_sem,
    sb_sem,
    rb_sem,
    sc_sem,
    rc_sem,
    sh_sem,
    rh_sem,
    sf_sem,
    rf_sem,
):
    loads, width = rhs_h.shape
    rows = width // 64
    ne = edges_v.shape[1]
    slots = ifr_v.shape[1]
    nc = fac_h.shape[1]
    wide_e = t_ref.shape[0] // loads
    me = lax.axis_index("sub")
    nxt = lax.rem(me + 1, n)
    prv = lax.rem(me + n - 1, n)
    lcols = ne * 64

    cp_rhs = pltpu.make_async_copy(rhs_h, r_ref, in_sem.at[0])
    cp_basis = pltpu.make_async_copy(basis_h, basis_st, in_sem.at[1])
    cp_fac = pltpu.make_async_copy(fac_h, fac_st, in_sem.at[2])
    cp_blk = pltpu.make_async_copy(blocks_h, stage_ref.at[:, pl.ds(0, lcols)], in_sem.at[3])
    cp_ifb = pltpu.make_async_copy(ifb_h, stage_ref.at[:, pl.ds(lcols, slots * 64)], in_sem.at[4])
    for cp in (cp_rhs, cp_basis, cp_fac, cp_blk, cp_ifb):
        cp.start()

    barrier = pltpu.get_barrier_semaphore()

    @pl.loop(1, n)
    def _(k):
        pl.semaphore_signal(barrier, inc=1, device_id={"sub": lax.rem(me + k, n)}, device_id_type=MESH)

    low_half = lax.broadcasted_iota(jnp.int32, (loads, 128), 1) < 64
    diagonal = lax.broadcasted_iota(jnp.int32, (loads, 128), 0) == lax.broadcasted_iota(jnp.int32, (loads, 128), 1)
    low_half64 = lax.broadcasted_iota(jnp.int32, (64, 128), 1) < 64
    own_block = (lax.broadcasted_iota(jnp.int32, (64, 256), 0) >> 4) == (lax.broadcasted_iota(jnp.int32, (64, 256), 1) >> 6)

    def lanes(i, size):
        return pl.ds(pl.multiple_of(i * size, size), size)

    def bcast(s):
        return jnp.broadcast_to(jnp.sum(s, axis=1, keepdims=True), (loads, 128))

    def split_into(src, dst, total, size):
        @pl.loop(0, total // size, unroll=2)
        def _(i):
            dst[:, lanes(i, size)] = stacked(src[:, lanes(i, size)])

    def contract(src, mat, total, size):
        def step(i, o):
            return o + dot_t(stacked(src[:, lanes(i, size)]), mat[:, lanes(i, size)])
        o = lax.fori_loop(0, total // size, step, jnp.zeros((2 * loads, 128), F32), unroll=2)
        return fold(o, loads)

    def send_parts(phase, coarse):
        lhs = stacked(coarse)

        @pl.loop(0, nc // 512, unroll=2)
        def _(i):
            o = dot(lhs, ff_ref[:, lanes(i, 512)])
            o = o[:loads] + o[loads:]
            for c in range(4):
                for h in range(2):
                    msg_a[phase, 8 * i + 2 * c + h] = o[8 * h : 8 * h + 8, 128 * c : 128 * c + 128]

        rcv_a[phase, me] = msg_a[phase, me]

        @pl.loop(1, n)
        def _(k):
            to = lax.rem(me + k, n)
            pltpu.make_async_remote_copy(
                msg_a.at[phase, to], rcv_a.at[phase, me], sa_sem.at[phase], ra_sem.at[phase],
                device_id={"sub": to}, device_id_type=MESH,
            ).start()

    def wait_all(buf, phase, sem):
        part = buf.at[phase, pl.ds(0, n - 1)]
        pltpu.make_async_copy(part, part, sem.at[phase]).wait()

    def pass_on(phase):
        wait_all(rcv_a, phase, ra_sem)
        tile = lax.fori_loop(0, n, lambda j, s: s + rcv_a[phase, j], jnp.zeros((8, 128), F32), unroll=8)
        msg_b[phase] = tile
        rcv_b[phase, me] = tile

        @pl.loop(1, n)
        def _(k):
            to = lax.rem(me + k, n)
            pltpu.make_async_remote_copy(
                msg_b.at[phase], rcv_b.at[phase, me], sb_sem.at[phase], rb_sem.at[phase],
                device_id={"sub": to}, device_id_type=MESH,
            ).start()

    def take_whole(phase, alpha):
        wait_all(rcv_b, phase, rb_sem)

        def step(m, norm):
            w = jnp.concatenate([rcv_b[phase, 2 * m], rcv_b[phase, 2 * m + 1]], axis=0)
            if alpha is not None:
                w = w_ref[:, lanes(m, 128)] - alpha * w
            w_ref[:, lanes(m, 128)] = w
            return norm + w * w

        return bcast(lax.fori_loop(0, n // 2, step, jnp.zeros((loads, 128), F32), unroll=4))

    def send_scalars(phase, s):
        line = jnp.sum(jnp.where(diagonal, bcast(s), 0.0), axis=0, keepdims=True)
        msg_c[phase] = line
        rcv_c[phase, me] = line

        @pl.loop(1, n)
        def _(k):
            to = lax.rem(me + k, n)
            pltpu.make_async_remote_copy(
                msg_c.at[phase], rcv_c.at[phase, me], sc_sem.at[phase], rc_sem.at[phase],
                device_id={"sub": to}, device_id_type=MESH,
            ).start()

    def take_scalars(phase):
        wait_all(rcv_c, phase, rc_sem)
        line = lax.fori_loop(0, n, lambda j, s: s + rcv_c[phase, j], jnp.zeros((1, 128), F32), unroll=8)
        return bcast(jnp.where(diagonal, jnp.broadcast_to(line, (loads, 128)), 0.0))

    def weighted(scale_ref, src):
        def step(i, s):
            v = src[:, lanes(i, 512)]
            v = scale_ref[:, lanes(i, 512)] * v * v
            return s + v[:, :128] + v[:, 128:256] + v[:, 256:384] + v[:, 384:]
        return lax.fori_loop(0, width // 512, step, jnp.zeros((loads, 128), F32), unroll=UNROLL)

    def precondition(visit):
        lhs = stacked(contract(w_ref, ff_ref, nc, 512))

        @pl.loop(0, width // 512, unroll=UNROLL)
        def _(i):
            o = dot(lhs, bs_ref[:, lanes(i, 512)])
            visit(i, jac_ref[:, lanes(i, 512)] * r_ref[:, lanes(i, 512)] + o[:loads] + o[loads:])

    def set_direction(i, p):
        p_ref[:, lanes(i, 512)] = p
        for c in range(4):
            a = p[:, 128 * c : 128 * c + 128]
            b = pltpu.roll(a, 64, 1)
            v_ref[8 * i + 2 * c] = jnp.where(low_half, a, b)
            v_ref[8 * i + 2 * c + 1] = jnp.where(low_half, b, a)

    def put_force(row, t):
        high = t.astype(BF16).astype(F32)
        t_ref[pl.ds(pl.multiple_of(row * loads, 16), t.shape[0]), :] = jnp.where(
            low_half64 if t.shape[0] == 64 else low_half, high, t - high
        )

    def force(diffs, cols):
        mats = [bb_ref[:, pl.ds(pl.multiple_of(col, 256), 256)] for col in cols]
        strains = [dot(stacked(d), b) for d, b in zip(diffs, mats)]
        strains = [jnp.where(own_block, u[:64] + u[64:], 0.0) for u in strains]
        forces = [fold(dot_t(stacked(u), b), 64) for u, b in zip(strains, mats)]
        squares = [u * u for u in strains]
        return forces, [u[0:16] + u[16:32] + u[32:48] + u[48:64] for u in squares]

    def local_groups(start, stop, acc):
        def step(i, acc):
            groups = [GROUPS * i + b for b in range(GROUPS)]
            diffs = []
            for g in groups:
                rows = [v_ref[edges_s[0, 4 * g + k]] - v_ref[edges_s[1, 4 * g + k]] for k in range(4)]
                diffs.append(jnp.concatenate(rows, axis=0))
            forces, energies = force(diffs, [256 * g for g in groups])
            for g, t in zip(groups, forces):
                put_force(4 * g, t)
            return acc + sum(energies)
        return lax.fori_loop(start // GROUPS, stop // GROUPS, step, acc)

    cp_rhs.wait()
    cp_basis.wait()
    split_into(basis_st, bs_ref, width, 512)
    coarse = contract(r_ref, bs_ref, width, 512)
    cp_fac.wait()
    split_into(fac_st, ff_ref, nc, 512)
    pl.semaphore_wait(barrier, n - 1)
    send_parts(0, coarse)
    send_scalars(0, weighted(jac_ref, r_ref))
    row_id = lax.broadcasted_iota(jnp.int32, (rows, ne), 0)
    inc_ref[...] = jnp.zeros_like(inc_ref)
    inc_ref[:, 0:ne] = ((row_id == edges_v[0:1, :]).astype(F32) - (row_id == edges_v[1:2, :]).astype(F32)).astype(BF16)
    row_id = lax.broadcasted_iota(jnp.int32, (rows, slots), 0)
    inc_ref[:, ne : ne + slots] = (row_id == ifr_v[...]).astype(F32).astype(BF16)
    inc_ref[:, ne + slots : ne + 2 * slots] = (-(row_id == snd_v[...]).astype(F32)).astype(BF16)
    used = (ne + 2 * slots) * loads
    if wide_e * loads > used:
        t_ref[used:, :] = jnp.zeros((wide_e * loads - used, 128), F32)

    pass_on(0)
    cp_blk.wait()
    cp_ifb.wait()
    split_into(stage_ref, bb_ref, stage_ref.shape[1], 512)
    gamma = take_whole(0, None) + take_scalars(0)
    precondition(set_direction)

    for it in range(ITERS):
        piece = slots * 8 // PIECES
        halos = []
        for c in range(PIECES):
            for k in range(c * slots // 2 // PIECES, (c + 1) * slots // 2 // PIECES):
                halo_s[it, 16 * k : 16 * k + 16, :] = jnp.where(
                    low_half, v_ref[snd_s[0, 2 * k]], v_ref[snd_s[0, 2 * k + 1]]
                )
            part = pl.ds(c * piece, piece)
            halos.append(pltpu.make_async_remote_copy(
                halo_s.at[it, part], halo_r.at[it, part], sh_sem.at[it, c], rh_sem.at[it, c],
                device_id={"sub": prv}, device_id_type=MESH,
            ))
            halos[-1].start()
        half = ne // 8
        acc = local_groups(0, half, jnp.zeros((loads, 256), F32))

        def interface(first, count):
            diffs = []
            for g in range(first, first + count):
                parts = []
                for a in range(2):
                    x = halo_r[it, 32 * g + 16 * a : 32 * g + 16 * a + 16, :]
                    y = pltpu.roll(x, 64, 1)
                    for b, there in enumerate((jnp.where(low_half, x, y), jnp.where(low_half, y, x))):
                        k = 4 * g + 2 * a + b
                        live = jnp.where(k < cnt_s[0], 1.0, 0.0).astype(F32)
                        parts.append((v_ref[ifr_s[0, k]] - there) * live)
                diffs.append(jnp.concatenate(parts, axis=0))
            forces, energies = force(diffs, [lcols + 256 * g for g in range(first, first + count)])
            for g, t in zip(range(first, first + count), forces):
                put_force(ne + 4 * g, t)
                for a in range(2):
                    frc_s[it, 32 * g + 16 * a : 32 * g + 16 * a + 16, :] = jnp.where(
                        low_half, t[32 * a : 32 * a + 16], t[32 * a + 16 : 32 * a + 32]
                    )
            return sum(energies)

        replies = []
        for c in range(PIECES):
            halos[c].wait()
            acc = acc + interface(c * slots // 4 // PIECES, slots // 4 // PIECES)
            part = pl.ds(c * piece, piece)
            replies.append(pltpu.make_async_remote_copy(
                frc_s.at[it, part], frc_r.at[it, part], sf_sem.at[it, c], rf_sem.at[it, c],
                device_id={"sub": nxt}, device_id_type=MESH,
            ))
            replies[-1].start()
        acc = local_groups(half, ne // 4, acc)
        energy = weighted(mass_ref, p_ref) + acc[:, :128] + acc[:, 128:]
        send_scalars(2 * it + 1, energy)
        for reply in replies:
            reply.wait()

        @pl.loop(0, slots // 2, unroll=UNROLL)
        def _(k):
            x = frc_r[it, pl.ds(pl.multiple_of(k * 16, 16), 16), :]
            y = pltpu.roll(x, 64, 1)
            put_force(ne + slots + 2 * k, jnp.where(low_half, x, y))
            put_force(ne + slots + 2 * k + 1, jnp.where(low_half, y, x))

        @pl.loop(0, loads // 2, unroll=2)
        def _(k):
            f = jnp.concatenate([t_ref[pl.ds(2 * k + h, wide_e, stride=loads), :] for h in range(2)], axis=1).astype(BF16)
            o = dot(inc_ref[...], f)
            for h in range(2):
                a = o[:, 128 * h : 128 * h + 128]
                qrow_ref[pl.ds(2 * k + h, rows, stride=loads), :] = a + pltpu.roll(a, 64, 1)

        def image(i, o):
            cols = []
            for c in range(4):
                pair = qrow_ref[pl.ds(pl.multiple_of((8 * i + 2 * c) * 16, 32), 32), :]
                cols.append(jnp.where(low_half, pair[:16], pair[16:]))
            q = mass_ref[:, lanes(i, 512)] * p_ref[:, lanes(i, 512)] + jnp.concatenate(cols, axis=1)
            q_ref[:, lanes(i, 512)] = q
            return o + dot_t(stacked(q), bs_ref[:, lanes(i, 512)])

        coarse = fold(lax.fori_loop(0, width // 512, image, jnp.zeros((2 * loads, 128), F32), unroll=UNROLL), loads)
        send_parts(it + 1, coarse)
        alpha = gamma / take_scalars(2 * it + 1)
        alpha4 = jnp.concatenate([alpha] * 4, axis=1)

        def update(i, s):
            r = r_ref[:, lanes(i, 512)] - alpha4 * q_ref[:, lanes(i, 512)]
            r_ref[:, lanes(i, 512)] = r
            v = jac_ref[:, lanes(i, 512)] * r * r
            return s + v[:, :128] + v[:, 128:256] + v[:, 256:384] + v[:, 384:]

        jr2 = lax.fori_loop(0, width // 512, update, jnp.zeros((loads, 128), F32), unroll=UNROLL)
        if it + 1 < ITERS:
            send_scalars(2 * it + 2, jr2)
        pass_on(it + 1)

        @pl.loop(0, width // 512, unroll=UNROLL)
        def _(i):
            step = alpha4 * p_ref[:, lanes(i, 512)]
            x_ref[:, lanes(i, 512)] = step if it == 0 else x_ref[:, lanes(i, 512)] + step

        norm = take_whole(it + 1, alpha)
        if it + 1 < ITERS:
            new = norm + take_scalars(2 * it + 2)
            beta4 = jnp.concatenate([new / gamma] * 4, axis=1)
            precondition(lambda i, z: set_direction(i, z + beta4 * p_ref[:, lanes(i, 512)]))
            gamma = new
        else:
            def finish(i, z):
                z_ref[:, lanes(i, 512)] = z
            precondition(finish)

    for phase in range(ITERS + 1):
        wait_all(rcv_a, phase, sa_sem)
        wait_all(rcv_b, phase, sb_sem)
    for phase in range(2 * ITERS):
        wait_all(rcv_c, phase, sc_sem)


def body(
    rhs,
    mass,
    jacobi,
    local_edges,
    local_blocks,
    if_rows,
    send_rows,
    if_count,
    if_blocks,
    coarse_basis,
    coarse_factor,
):
    n = lax.axis_size("sub")
    loads, width = rhs.shape
    ne = local_edges.shape[1]
    slots = if_rows.shape[0]
    nc = coarse_factor.shape[1]
    rows = width // 64
    wide_e = -(-(ne + 2 * slots) // 128) * 128
    cols = (ne + slots) * 64
    phases = ITERS + 1
    vmem = pl.BlockSpec(memory_space=pltpu.VMEM)
    smem = pl.BlockSpec(memory_space=pltpu.SMEM)
    hbm = pl.BlockSpec(memory_space=pl.ANY)
    dma = pltpu.SemaphoreType.DMA
    if_rows = if_rows.reshape(1, slots)
    send_rows = send_rows.reshape(1, slots)
    out = jax.ShapeDtypeStruct((loads, width), F32)
    return pl.pallas_call(
        functools.partial(kernel, n),
        out_shape=(out, out),
        in_specs=[vmem] * 2 + [smem] * 4 + [vmem] * 3 + [hbm] * 5,
        out_specs=(vmem, vmem),
        scratch_shapes=[
            pltpu.VMEM((loads, width), F32),
            pltpu.VMEM((loads, width), F32),
            pltpu.VMEM((loads, width), F32),
            pltpu.VMEM((rows, loads, 128), F32),
            pltpu.VMEM((rows * loads, 128), F32),
            pltpu.VMEM((wide_e * loads, 128), F32),
            pltpu.VMEM((rows, wide_e), BF16),
            pltpu.VMEM((64, cols), F32),
            pltpu.VMEM((64, width), F32),
            pltpu.VMEM((64, nc), F32),
            pltpu.VMEM((128, cols), BF16),
            pltpu.VMEM((128, width), BF16),
            pltpu.VMEM((128, nc), BF16),
            pltpu.VMEM((loads, nc), F32),
            pltpu.VMEM((phases, n, 8, 128), F32),
            pltpu.VMEM((phases, n, 8, 128), F32),
            pltpu.VMEM((phases, 8, 128), F32),
            pltpu.VMEM((phases, n, 8, 128), F32),
            pltpu.VMEM((2 * ITERS, 1, 128), F32),
            pltpu.VMEM((2 * ITERS, n, 1, 128), F32),
            pltpu.VMEM((ITERS, slots * 8, 128), F32),
            pltpu.VMEM((ITERS, slots * 8, 128), F32),
            pltpu.VMEM((ITERS, slots * 8, 128), F32),
            pltpu.VMEM((ITERS, slots * 8, 128), F32),
            dma((5,)),
            dma((phases,)),
            dma((phases,)),
            dma((phases,)),
            dma((phases,)),
            dma((2 * ITERS,)),
            dma((2 * ITERS,)),
            dma((ITERS, PIECES)),
            dma((ITERS, PIECES)),
            dma((ITERS, PIECES)),
            dma((ITERS, PIECES)),
        ],
        compiler_params=pltpu.CompilerParams(collective_id=0, has_side_effects=True, vmem_limit_bytes=56 * 2**20),
    )(
        mass.reshape(1, width),
        jacobi.reshape(1, width),
        local_edges,
        if_rows,
        send_rows,
        if_count,
        local_edges,
        if_rows,
        send_rows,
        rhs,
        local_blocks,
        if_blocks,
        coarse_basis,
        coarse_factor,
    )


def solution(mesh):
    in_specs = (
        P("groups", "sub"),
        P(("groups", "sub")),
        P(("groups", "sub")),
        P(None, ("groups", "sub")),
        P(None, ("groups", "sub")),
        P(("groups", "sub")),
        P(("groups", "sub")),
        P(("groups", "sub")),
        P(None, ("groups", "sub")),
        P(None, ("groups", "sub")),
        P(("groups", "sub"), None),
    )
    out_specs = (P("groups", "sub"), P("groups", "sub"))
    return jax.shard_map(body, mesh=mesh, in_specs=in_specs, out_specs=out_specs, check_vma=False)
```

```python
import functools

import jax
import jax.numpy as jnp
from jax import lax
from jax.experimental import pallas as pl
from jax.experimental.pallas import tpu as pltpu
from jax.sharding import PartitionSpec as P

ITERS = 2
F32 = jnp.float32
BF16 = jnp.bfloat16
MESH = pl.DeviceIdType.MESH
GROUPS = 8
PIECES = 2
UNROLL = 4


def split(x):
    high = x.astype(BF16)
    return high, (x - high.astype(F32)).astype(BF16)


def stacked(x):
    high, low = split(x)
    return jnp.concatenate([high, low], axis=0)


def dot(a, b):
    return jnp.dot(a, b, preferred_element_type=F32)


def dot_t(a, b):
    return lax.dot_general(a, b, (((1,), (1,)), ((), ())), preferred_element_type=F32)


def fold(o, rows):
    a = o[:rows] + o[rows:]
    return a + pltpu.roll(a, 64, 1)


def kernel(
    n,
    mass_ref,
    jac_ref,
    edges_s,
    ifr_s,
    snd_s,
    cnt_s,
    edges_v,
    ifr_v,
    snd_v,
    rhs_h,
    blocks_h,
    ifb_h,
    basis_h,
    fac_h,
    x_ref,
    z_ref,
    r_ref,
    p_ref,
    q_ref,
    v_ref,
    qrow_ref,
    t_ref,
    inc_ref,
    stage_ref,
    basis_st,
    fac_st,
    bb_ref,
    bs_ref,
    ff_ref,
    w_ref,
    msg_a,
    rcv_a,
    msg_b,
    rcv_b,
    msg_c,
    rcv_c,
    halo_s,
    halo_r,
    frc_s,
    frc_r,
    in_sem,
    sa_sem,
    ra_sem,
    sb_sem,
    rb_sem,
    sc_sem,
    rc_sem,
    sh_sem,
    rh_sem,
    sf_sem,
    rf_sem,
):
    loads, width = rhs_h.shape
    rows = width // 64
    ne = edges_v.shape[1]
    slots = ifr_v.shape[1]
    nc = fac_h.shape[1]
    wide_e = t_ref.shape[0] // loads
    me = lax.axis_index("sub")
    nxt = lax.rem(me + 1, n)
    prv = lax.rem(me + n - 1, n)
    lcols = ne * 64

    cp_rhs = pltpu.make_async_copy(rhs_h, r_ref, in_sem.at[0])
    cp_basis = pltpu.make_async_copy(basis_h, basis_st, in_sem.at[1])
    cp_fac = pltpu.make_async_copy(fac_h, fac_st, in_sem.at[2])
    cp_blk = pltpu.make_async_copy(blocks_h, stage_ref.at[:, pl.ds(0, lcols)], in_sem.at[3])
    cp_ifb = pltpu.make_async_copy(ifb_h, stage_ref.at[:, pl.ds(lcols, slots * 64)], in_sem.at[4])
    for cp in (cp_rhs, cp_basis, cp_fac, cp_blk, cp_ifb):
        cp.start()

    barrier = pltpu.get_barrier_semaphore()

    @pl.loop(1, n)
    def _(k):
        pl.semaphore_signal(barrier, inc=1, device_id={"sub": lax.rem(me + k, n)}, device_id_type=MESH)

    low_half = lax.broadcasted_iota(jnp.int32, (loads, 128), 1) < 64
    diagonal = lax.broadcasted_iota(jnp.int32, (loads, 128), 0) == lax.broadcasted_iota(jnp.int32, (loads, 128), 1)
    low_half64 = lax.broadcasted_iota(jnp.int32, (64, 128), 1) < 64
    own_block = (lax.broadcasted_iota(jnp.int32, (64, 256), 0) >> 4) == (lax.broadcasted_iota(jnp.int32, (64, 256), 1) >> 6)

    def lanes(i, size):
        return pl.ds(pl.multiple_of(i * size, size), size)

    def bcast(s):
        return jnp.broadcast_to(jnp.sum(s, axis=1, keepdims=True), (loads, 128))

    def split_into(src, dst, total, size):
        @pl.loop(0, total // size, unroll=2)
        def _(i):
            dst[:, lanes(i, size)] = stacked(src[:, lanes(i, size)])

    def contract(src, mat, total, size):
        def step(i, o):
            return o + dot_t(stacked(src[:, lanes(i, size)]), mat[:, lanes(i, size)])
        o = lax.fori_loop(0, total // size, step, jnp.zeros((2 * loads, 128), F32), unroll=2)
        return fold(o, loads)

    def send_parts(phase, coarse):
        lhs = stacked(coarse)

        @pl.loop(0, nc // 512, unroll=2)
        def _(i):
            o = dot(lhs, ff_ref[:, lanes(i, 512)])
            o = o[:loads] + o[loads:]
            for c in range(4):
                for h in range(2):
                    msg_a[phase, 8 * i + 2 * c + h] = o[8 * h : 8 * h + 8, 128 * c : 128 * c + 128]

        rcv_a[phase, me] = msg_a[phase, me]

        @pl.loop(1, n)
        def _(k):
            to = lax.rem(me + k, n)
            pltpu.make_async_remote_copy(
                msg_a.at[phase, to], rcv_a.at[phase, me], sa_sem.at[phase], ra_sem.at[phase],
                device_id={"sub": to}, device_id_type=MESH,
            ).start()

    def wait_all(buf, phase, sem):
        part = buf.at[phase, pl.ds(0, n - 1)]
        pltpu.make_async_copy(part, part, sem.at[phase]).wait()

    def pass_on(phase):
        wait_all(rcv_a, phase, ra_sem)
        tile = lax.fori_loop(0, n, lambda j, s: s + rcv_a[phase, j], jnp.zeros((8, 128), F32), unroll=8)
        msg_b[phase] = tile
        rcv_b[phase, me] = tile

        @pl.loop(1, n)
        def _(k):
            to = lax.rem(me + k, n)
            pltpu.make_async_remote_copy(
                msg_b.at[phase], rcv_b.at[phase, me], sb_sem.at[phase], rb_sem.at[phase],
                device_id={"sub": to}, device_id_type=MESH,
            ).start()

    def take_whole(phase, alpha):
        wait_all(rcv_b, phase, rb_sem)

        def step(m, norm):
            w = jnp.concatenate([rcv_b[phase, 2 * m], rcv_b[phase, 2 * m + 1]], axis=0)
            if alpha is not None:
                w = w_ref[:, lanes(m, 128)] - alpha * w
            w_ref[:, lanes(m, 128)] = w
            return norm + w * w

        return bcast(lax.fori_loop(0, n // 2, step, jnp.zeros((loads, 128), F32), unroll=4))

    def send_scalars(phase, s):
        line = jnp.sum(jnp.where(diagonal, bcast(s), 0.0), axis=0, keepdims=True)
        msg_c[phase] = line
        rcv_c[phase, me] = line

        @pl.loop(1, n)
        def _(k):
            to = lax.rem(me + k, n)
            pltpu.make_async_remote_copy(
                msg_c.at[phase], rcv_c.at[phase, me], sc_sem.at[phase], rc_sem.at[phase],
                device_id={"sub": to}, device_id_type=MESH,
            ).start()

    def take_scalars(phase):
        wait_all(rcv_c, phase, rc_sem)
        line = lax.fori_loop(0, n, lambda j, s: s + rcv_c[phase, j], jnp.zeros((1, 128), F32), unroll=8)
        return bcast(jnp.where(diagonal, jnp.broadcast_to(line, (loads, 128)), 0.0))

    def weighted(scale_ref, src):
        def step(i, s):
            v = src[:, lanes(i, 512)]
            v = scale_ref[:, lanes(i, 512)] * v * v
            return s + v[:, :128] + v[:, 128:256] + v[:, 256:384] + v[:, 384:]
        return lax.fori_loop(0, width // 512, step, jnp.zeros((loads, 128), F32), unroll=UNROLL)

    def precondition(visit):
        lhs = stacked(contract(w_ref, ff_ref, nc, 512))

        @pl.loop(0, width // 512, unroll=UNROLL)
        def _(i):
            o = dot(lhs, bs_ref[:, lanes(i, 512)])
            visit(i, jac_ref[:, lanes(i, 512)] * r_ref[:, lanes(i, 512)] + o[:loads] + o[loads:])

    def set_direction(i, p):
        p_ref[:, lanes(i, 512)] = p
        for c in range(4):
            a = p[:, 128 * c : 128 * c + 128]
            b = pltpu.roll(a, 64, 1)
            v_ref[8 * i + 2 * c] = jnp.where(low_half, a, b)
            v_ref[8 * i + 2 * c + 1] = jnp.where(low_half, b, a)

    def put_force(row, t):
        high = t.astype(BF16).astype(F32)
        t_ref[pl.ds(pl.multiple_of(row * loads, 16), t.shape[0]), :] = jnp.where(
            low_half64 if t.shape[0] == 64 else low_half, high, t - high
        )

    def force(diffs, cols):
        mats = [bb_ref[:, pl.ds(pl.multiple_of(col, 256), 256)] for col in cols]
        strains = [dot(stacked(d), b) for d, b in zip(diffs, mats)]
        strains = [jnp.where(own_block, u[:64] + u[64:], 0.0) for u in strains]
        forces = [fold(dot_t(stacked(u), b), 64) for u, b in zip(strains, mats)]
        squares = [u * u for u in strains]
        return forces, [u[0:16] + u[16:32] + u[32:48] + u[48:64] for u in squares]

    def local_groups(start, stop, acc):
        def step(i, acc):
            groups = [GROUPS * i + b for b in range(GROUPS)]
            diffs = []
            for g in groups:
                rows = [v_ref[edges_s[0, 4 * g + k]] - v_ref[edges_s[1, 4 * g + k]] for k in range(4)]
                diffs.append(jnp.concatenate(rows, axis=0))
            forces, energies = force(diffs, [256 * g for g in groups])
            for g, t in zip(groups, forces):
                put_force(4 * g, t)
            return acc + sum(energies)
        return lax.fori_loop(start // GROUPS, stop // GROUPS, step, acc)

    cp_rhs.wait()
    cp_basis.wait()
    split_into(basis_st, bs_ref, width, 512)
    coarse = contract(r_ref, bs_ref, width, 512)
    cp_fac.wait()
    split_into(fac_st, ff_ref, nc, 512)
    pl.semaphore_wait(barrier, n - 1)
    send_parts(0, coarse)
    send_scalars(0, weighted(jac_ref, r_ref))
    row_id = lax.broadcasted_iota(jnp.int32, (rows, ne), 0)
    inc_ref[...] = jnp.zeros_like(inc_ref)
    inc_ref[:, 0:ne] = ((row_id == edges_v[0:1, :]).astype(F32) - (row_id == edges_v[1:2, :]).astype(F32)).astype(BF16)
    row_id = lax.broadcasted_iota(jnp.int32, (rows, slots), 0)
    inc_ref[:, ne : ne + slots] = (row_id == ifr_v[...]).astype(F32).astype(BF16)
    inc_ref[:, ne + slots : ne + 2 * slots] = (-(row_id == snd_v[...]).astype(F32)).astype(BF16)
    used = (ne + 2 * slots) * loads
    if wide_e * loads > used:
        t_ref[used:, :] = jnp.zeros((wide_e * loads - used, 128), F32)

    pass_on(0)
    cp_blk.wait()
    cp_ifb.wait()
    split_into(stage_ref, bb_ref, stage_ref.shape[1], 512)
    gamma = take_whole(0, None) + take_scalars(0)
    precondition(set_direction)

    for it in range(ITERS):
        piece = slots * 8 // PIECES
        halos = []
        for c in range(PIECES):
            for k in range(c * slots // 2 // PIECES, (c + 1) * slots // 2 // PIECES):
                halo_s[it, 16 * k : 16 * k + 16, :] = jnp.where(
                    low_half, v_ref[snd_s[0, 2 * k]], v_ref[snd_s[0, 2 * k + 1]]
                )
            part = pl.ds(c * piece, piece)
            halos.append(pltpu.make_async_remote_copy(
                halo_s.at[it, part], halo_r.at[it, part], sh_sem.at[it, c], rh_sem.at[it, c],
                device_id={"sub": prv}, device_id_type=MESH,
            ))
            halos[-1].start()
        half = ne // 8
        acc = local_groups(0, half, jnp.zeros((loads, 256), F32))

        def interface(first, count):
            diffs = []
            for g in range(first, first + count):
                parts = []
                for a in range(2):
                    x = halo_r[it, 32 * g + 16 * a : 32 * g + 16 * a + 16, :]
                    y = pltpu.roll(x, 64, 1)
                    for b, there in enumerate((jnp.where(low_half, x, y), jnp.where(low_half, y, x))):
                        k = 4 * g + 2 * a + b
                        live = jnp.where(k < cnt_s[0], 1.0, 0.0).astype(F32)
                        parts.append((v_ref[ifr_s[0, k]] - there) * live)
                diffs.append(jnp.concatenate(parts, axis=0))
            forces, energies = force(diffs, [lcols + 256 * g for g in range(first, first + count)])
            for g, t in zip(range(first, first + count), forces):
                put_force(ne + 4 * g, t)
                for a in range(2):
                    frc_s[it, 32 * g + 16 * a : 32 * g + 16 * a + 16, :] = jnp.where(
                        low_half, t[32 * a : 32 * a + 16], t[32 * a + 16 : 32 * a + 32]
                    )
            return sum(energies)

        replies = []
        for c in range(PIECES):
            halos[c].wait()
            acc = acc + interface(c * slots // 4 // PIECES, slots // 4 // PIECES)
            part = pl.ds(c * piece, piece)
            replies.append(pltpu.make_async_remote_copy(
                frc_s.at[it, part], frc_r.at[it, part], sf_sem.at[it, c], rf_sem.at[it, c],
                device_id={"sub": nxt}, device_id_type=MESH,
            ))
            replies[-1].start()
        acc = local_groups(half, ne // 4, acc)
        energy = weighted(mass_ref, p_ref) + acc[:, :128] + acc[:, 128:]
        send_scalars(2 * it + 1, energy)
        for reply in replies:
            reply.wait()

        @pl.loop(0, slots // 2, unroll=UNROLL)
        def _(k):
            x = frc_r[it, pl.ds(pl.multiple_of(k * 16, 16), 16), :]
            y = pltpu.roll(x, 64, 1)
            put_force(ne + slots + 2 * k, jnp.where(low_half, x, y))
            put_force(ne + slots + 2 * k + 1, jnp.where(low_half, y, x))

        @pl.loop(0, loads // 2, unroll=2)
        def _(k):
            f = jnp.concatenate([t_ref[pl.ds(2 * k + h, wide_e, stride=loads), :] for h in range(2)], axis=1).astype(BF16)
            o = dot(inc_ref[...], f)
            for h in range(2):
                a = o[:, 128 * h : 128 * h + 128]
                qrow_ref[pl.ds(2 * k + h, rows, stride=loads), :] = a + pltpu.roll(a, 64, 1)

        def image(i, o):
            cols = []
            for c in range(4):
                pair = qrow_ref[pl.ds(pl.multiple_of((8 * i + 2 * c) * 16, 32), 32), :]
                cols.append(jnp.where(low_half, pair[:16], pair[16:]))
            q = mass_ref[:, lanes(i, 512)] * p_ref[:, lanes(i, 512)] + jnp.concatenate(cols, axis=1)
            q_ref[:, lanes(i, 512)] = q
            return o + dot_t(stacked(q), bs_ref[:, lanes(i, 512)])

        coarse = fold(lax.fori_loop(0, width // 512, image, jnp.zeros((2 * loads, 128), F32), unroll=UNROLL), loads)
        send_parts(it + 1, coarse)
        alpha = gamma / take_scalars(2 * it + 1)
        alpha4 = jnp.concatenate([alpha] * 4, axis=1)

        def update(i, s):
            r = r_ref[:, lanes(i, 512)] - alpha4 * q_ref[:, lanes(i, 512)]
            r_ref[:, lanes(i, 512)] = r
            v = jac_ref[:, lanes(i, 512)] * r * r
            return s + v[:, :128] + v[:, 128:256] + v[:, 256:384] + v[:, 384:]

        jr2 = lax.fori_loop(0, width // 512, update, jnp.zeros((loads, 128), F32), unroll=UNROLL)
        if it + 1 < ITERS:
            send_scalars(2 * it + 2, jr2)
        pass_on(it + 1)

        @pl.loop(0, width // 512, unroll=UNROLL)
        def _(i):
            step = alpha4 * p_ref[:, lanes(i, 512)]
            x_ref[:, lanes(i, 512)] = step if it == 0 else x_ref[:, lanes(i, 512)] + step

        norm = take_whole(it + 1, alpha)
        if it + 1 < ITERS:
            new = norm + take_scalars(2 * it + 2)
            beta4 = jnp.concatenate([new / gamma] * 4, axis=1)
            precondition(lambda i, z: set_direction(i, z + beta4 * p_ref[:, lanes(i, 512)]))
            gamma = new
        else:
            def finish(i, z):
                z_ref[:, lanes(i, 512)] = z
            precondition(finish)

    for phase in range(ITERS + 1):
        wait_all(rcv_a, phase, sa_sem)
        wait_all(rcv_b, phase, sb_sem)
    for phase in range(2 * ITERS):
        wait_all(rcv_c, phase, sc_sem)


def hand_over(x_ref, z_ref, x_out, z_out):
    x_out[...] = x_ref[...]
    z_out[...] = z_ref[...]


def body(
    rhs,
    mass,
    jacobi,
    local_edges,
    local_blocks,
    if_rows,
    send_rows,
    if_count,
    if_blocks,
    coarse_basis,
    coarse_factor,
):
    n = lax.axis_size("sub")
    loads, width = rhs.shape
    ne = local_edges.shape[1]
    slots = if_rows.shape[0]
    nc = coarse_factor.shape[1]
    rows = width // 64
    wide_e = -(-(ne + 2 * slots) // 128) * 128
    cols = (ne + slots) * 64
    phases = ITERS + 1
    vmem = pl.BlockSpec(memory_space=pltpu.VMEM)
    smem = pl.BlockSpec(memory_space=pltpu.SMEM)
    hbm = pl.BlockSpec(memory_space=pl.ANY)
    dma = pltpu.SemaphoreType.DMA
    if_rows = if_rows.reshape(1, slots)
    send_rows = send_rows.reshape(1, slots)
    out = jax.ShapeDtypeStruct((loads, width), F32)
    result = pl.pallas_call(
        functools.partial(kernel, n),
        out_shape=(out, out),
        in_specs=[vmem] * 2 + [smem] * 4 + [vmem] * 3 + [hbm] * 5,
        out_specs=(vmem, vmem),
        scratch_shapes=[
            pltpu.VMEM((loads, width), F32),
            pltpu.VMEM((loads, width), F32),
            pltpu.VMEM((loads, width), F32),
            pltpu.VMEM((rows, loads, 128), F32),
            pltpu.VMEM((rows * loads, 128), F32),
            pltpu.VMEM((wide_e * loads, 128), F32),
            pltpu.VMEM((rows, wide_e), BF16),
            pltpu.VMEM((64, cols), F32),
            pltpu.VMEM((64, width), F32),
            pltpu.VMEM((64, nc), F32),
            pltpu.VMEM((128, cols), BF16),
            pltpu.VMEM((128, width), BF16),
            pltpu.VMEM((128, nc), BF16),
            pltpu.VMEM((loads, nc), F32),
            pltpu.VMEM((phases, n, 8, 128), F32),
            pltpu.VMEM((phases, n, 8, 128), F32),
            pltpu.VMEM((phases, 8, 128), F32),
            pltpu.VMEM((phases, n, 8, 128), F32),
            pltpu.VMEM((2 * ITERS, 1, 128), F32),
            pltpu.VMEM((2 * ITERS, n, 1, 128), F32),
            pltpu.VMEM((ITERS, slots * 8, 128), F32),
            pltpu.VMEM((ITERS, slots * 8, 128), F32),
            pltpu.VMEM((ITERS, slots * 8, 128), F32),
            pltpu.VMEM((ITERS, slots * 8, 128), F32),
            dma((5,)),
            dma((phases,)),
            dma((phases,)),
            dma((phases,)),
            dma((phases,)),
            dma((2 * ITERS,)),
            dma((2 * ITERS,)),
            dma((ITERS, PIECES)),
            dma((ITERS, PIECES)),
            dma((ITERS, PIECES)),
            dma((ITERS, PIECES)),
        ],
        compiler_params=pltpu.CompilerParams(collective_id=0, has_side_effects=True, vmem_limit_bytes=56 * 2**20),
    )(
        mass.reshape(1, width),
        jacobi.reshape(1, width),
        local_edges,
        if_rows,
        send_rows,
        if_count,
        local_edges,
        if_rows,
        send_rows,
        rhs,
        local_blocks,
        if_blocks,
        coarse_basis,
        coarse_factor,
    )
    return pl.pallas_call(
        hand_over,
        grid=(2,),
        out_shape=(out, out),
        in_specs=[pl.BlockSpec((loads, width // 2), lambda i: (0, i))] * 2,
        out_specs=[pl.BlockSpec((loads, width // 2), lambda i: (0, i))] * 2,
    )(*result)


def solution(mesh):
    in_specs = (
        P("groups", "sub"),
        P(("groups", "sub")),
        P(("groups", "sub")),
        P(None, ("groups", "sub")),
        P(None, ("groups", "sub")),
        P(("groups", "sub")),
        P(("groups", "sub")),
        P(("groups", "sub")),
        P(None, ("groups", "sub")),
        P(None, ("groups", "sub")),
        P(("groups", "sub"), None),
    )
    out_specs = (P("groups", "sub"), P("groups", "sub"))
    return jax.shard_map(body, mesh=mesh, in_specs=in_specs, out_specs=out_specs, check_vma=False)
```
